32 devices in a mesh: row: 8 (over y, x, core), col: 4 (over z).
Axes of the slice: x: 2, y: 2, z: 4, core: 2. Of those that a mesh axis runs over, the one named last changes fastest.
Arguments:
- counts: int32 [8192, 8192], P('row', 'col'), may hold values from 0 to 33, as said below
- row_emb: float32 [256, 8192], P('col', 'row'), may hold values from -2 to 2
- col_emb: float32 [256, 8192], P('row', 'col'), may hold values from -2 to 2
- row_accum: float32 [256, 8192], P('col', 'row'), may hold values from 100 to 10000
- col_accum: float32 [256, 8192], P('row', 'col'), may hold values from 100 to 10000
Outputs:
- new_row_emb: float32 [256, 8192], P('col', 'row')
- new_col_emb: float32 [256, 8192], P('row', 'col')
The draws below stay inside these ranges and needn't reach their ends.
Inputs may be any that keep to these rules, and one draw needn't show every extreme that they name: `counts`: every row word and every column word has a positive count with some partner.
All inputs are finite; a program needn't handle non-finite values.
Results may differ from the reference program's by a relative error of at most 0.0015.
Values may be sent and summed in bfloat16 or wider, within the bound.
A program may use at most 64 MiB of HBM per device.

```python
import math
import jax
import jax.numpy as jnp
from jax import lax

D = 256
BR = 1024
SWEEPS = 2
NR = 8192
NC = 8192
N_ROW = 8


def draw_counts(key, part):
    first = jax.random.fold_in(key, 11)
    second = jax.random.fold_in(key, 23)
    rows_idx = jnp.arange(NR, dtype=jnp.int32)[:, None]
    cols_idx = jnp.arange(NC, dtype=jnp.int32)[None, :]
    power = 4 * rows_idx // NR + 3 * cols_idx // NC
    ceiling = 2 + jnp.left_shift(jnp.ones_like(power), power)
    values = jax.random.randint(first, (NR, NC), 0, ceiling)
    keeper = jax.random.randint(second, (NR, NC), 0, 2)
    values = values * keeper
    forced = rows_idx % 64 == cols_idx % 64
    corner = (rows_idx == NR - 1) & (cols_idx == NC - 1)
    values = jnp.where(forced, jnp.maximum(values, 1), values)
    values = jnp.where(corner, 33, values)
    return values.astype(jnp.int32)


def steps_of(rng, shape, pieces, least, top_value):
    level, own = 1.0, jax.random.fold_in(rng, 6)
    for axis_at, blocks in pieces:
        heights = jnp.exp(jax.random.uniform(jax.random.fold_in(own, axis_at), (blocks,), jnp.float32, least / len(pieces), top_value / len(pieces)))
        level = level * jnp.repeat(heights, shape[axis_at] // blocks).reshape([-1 if axis == axis_at else 1 for axis in range(len(shape))])
    return level


def bell_draw(own_key, dims, width, most, shards=(), kind=jnp.bfloat16):
    gain = steps_of(own_key, dims, shards, -0.22, 0.18) if shards else 1.0
    entries = jax.random.normal(own_key, dims, jnp.float32) * width * gain
    return jnp.minimum(jnp.maximum(entries, -most), most).astype(kind)


def setup_inputs(seed: int = 0) -> dict:
    splits = jax.random.split(jax.random.key(seed), 6)
    return {
        "counts": draw_counts(jax.random.fold_in(splits[5], 71), 0),
        "row_emb": bell_draw(splits[1], (D, NR), 0.3, 2.0, ((0, 4), (1, 8)), jnp.float32),
        "col_emb": bell_draw(splits[2], (D, NC), 0.3, 2.0, ((0, 8), (1, 4)), jnp.float32),
        "row_accum": jnp.clip(jnp.exp(math.log(10000.0) - 4.6051702 * jax.random.uniform(splits[3], (D, NR), jnp.float32) ** steps_of(splits[3], (D, NR), ((0, 4), (1, 8)), -0.2, 0.2)), 100.0, 10000.0),
        "col_accum": jnp.clip(jnp.exp(math.log(10000.0) - 4.6051702 * jax.random.uniform(splits[4], (D, NC), jnp.float32) ** steps_of(splits[4], (D, NC), ((0, 8), (1, 4)), -0.2, 0.2)), 100.0, 10000.0),
    }


def reference(counts, row_emb, col_emb, row_accum, col_accum):
    blocks = counts.reshape(N_ROW, BR, NC)

    def margins(block):
        values = block.astype(jnp.float32)
        return (lax.optimization_barrier(jnp.sum(values, axis=1)), lax.optimization_barrier(jnp.sum(values, axis=0)))
    row_parts, col_parts = lax.map(margins, blocks)
    row_marg = row_parts.reshape(NR)
    col_marg = lax.optimization_barrier(jnp.sum(col_parts, axis=0))
    total = jnp.sum(row_marg)
    log_total = jnp.log(total)
    log_rows = jnp.log(row_marg).reshape(N_ROW, BR)
    log_cols = jnp.log(col_marg)
    for sweep in range(SWEEPS):
        row_half = row_emb.astype(jnp.bfloat16)
        col_half = col_emb.astype(jnp.bfloat16)

        def step(carry, index):
            block = lax.dynamic_index_in_dim(blocks, index, 0, False)
            log_row = lax.dynamic_index_in_dim(log_rows, index, 0, False)
            values = block.astype(jnp.float32)
            target = jnp.log(jnp.maximum(values, 1.0)) + log_total - log_row[:, None] - log_cols[None, :]
            weight = 0.1 + 0.25 * jnp.sqrt(values)
            row_part = lax.dynamic_slice_in_dim(row_half, (index * BR).astype(jnp.int32), BR, 1)
            scores = lax.dot_general(row_part, col_half, (((0,), (0,)), ((), ())), preferred_element_type=jnp.float32)
            errors = scores - target
            grads = jnp.where(block > 0, weight * errors, jax.nn.sigmoid(errors)).astype(jnp.bfloat16)
            row_grad = lax.dot_general(col_half, grads, (((1,), (1,)), ((), ())), preferred_element_type=jnp.float32)
            col_grad = carry + jnp.dot(row_part, grads, preferred_element_type=jnp.float32)
            return (col_grad, row_grad)
        col_grad, row_stack = lax.scan(step, jnp.zeros((D, NC), jnp.float32), jnp.arange(N_ROW, dtype=jnp.int32))
        row_grad = jnp.transpose(row_stack, (1, 0, 2)).reshape(D, NR)
        row_accum = row_accum + row_grad * row_grad
        row_emb = row_emb - 0.05 * row_grad / jnp.sqrt(row_accum)
        col_accum = col_accum + col_grad * col_grad
        col_emb = col_emb - 0.05 * col_grad / jnp.sqrt(col_accum)
    return (row_emb, col_emb)
```

```python
import functools

import jax
import jax.numpy as jnp
from jax import lax
from jax.experimental import pallas as pl
from jax.experimental.pallas import tpu as pltpu
from jax.sharding import PartitionSpec as P

SWEEPS = 2
ROW_CHUNKS = 4
COL_CHUNKS = 4
MESH = pl.DeviceIdType.MESH
F32 = jnp.float32
BF16 = jnp.bfloat16


def kernel(
    n_row, n_col, counts_hbm, row_emb_in, col_emb_in, row_acc_in, col_acc_in, row_out, col_out,
    counts, base, weight, grads, row_shift, col_shift, row_stat, col_stat, tot_stat,
    row_blk, col_blk, row_part, col_part, row_recv, col_recv, row_acc, col_acc,
    load_sem, rs_send, rs_recv, cs_send, cs_recv, ts_send, ts_recv,
    rg_send, rg_recv, cg_send, cg_recv, rr_send, rr_recv, cr_send, cr_recv,
):
    me_r, me_c = lax.axis_index("row"), lax.axis_index("col")
    br, bc = counts.shape
    dr, dc = row_emb_in.shape[0], col_emb_in.shape[0]
    d = dr * n_col
    cr, cc = br // ROW_CHUNKS, bc // COL_CHUNKS

    def peer(axis, k):
        return lax.rem(me_r + k, n_row) if axis == "row" else lax.rem(me_c + k, n_col)

    def copy(axis, k, src, dst, send_sem, recv_sem):
        return pltpu.make_async_remote_copy(
            src_ref=src, dst_ref=dst, send_sem=send_sem, recv_sem=recv_sem,
            device_id={axis: peer(axis, k)}, device_id_type=MESH,
        )

    def load(c):
        rows = pl.ds(pl.multiple_of(c * cr, cr), cr)
        return pltpu.make_async_copy(counts_hbm.at[rows, :], counts.at[rows, :], load_sem.at[c])

    def rcols(c):
        return pl.ds(pl.multiple_of(c * cr, cr), cr)

    def ccols(c):
        return pl.ds(pl.multiple_of(c * cc, cc), cc)

    def row_gather(s, c, k):
        own = row_blk.at[s, me_c, :, rcols(c)]
        return copy("col", k, own, own, rg_send.at[s, c, k], rg_recv.at[s, c, me_c])

    def row_gather_in(s, c, k):
        p = peer("col", k)
        slot = row_blk.at[s, p, :, rcols(c)]
        return copy("col", k, slot, slot, rg_send.at[s, c, k], rg_recv.at[s, c, p])

    def col_gather(s, c, k):
        own = col_blk.at[s, me_r, :, ccols(c)]
        return copy("row", k, own, own, cg_send.at[s, c, k], cg_recv.at[s, c, me_r])

    def col_gather_in(s, c, k):
        p = peer("row", k)
        slot = col_blk.at[s, p, :, ccols(c)]
        return copy("row", k, slot, slot, cg_send.at[s, c, k], cg_recv.at[s, c, p])

    def row_reduce(s, c, k):
        return copy(
            "col", k, row_part.at[s, peer("col", k), :, rcols(c)], row_recv.at[s, me_c, :, rcols(c)],
            rr_send.at[s, c, k], rr_recv.at[s, c, me_c],
        )

    def row_reduce_in(s, c, k):
        p = peer("col", k)
        slot = row_recv.at[s, p, :, rcols(c)]
        return copy("col", k, slot, slot, rr_send.at[s, c, k], rr_recv.at[s, c, p])

    def col_reduce(s, c, k):
        return copy(
            "row", k, col_part.at[s, peer("row", k), :, ccols(c)], col_recv.at[s, me_r, :, ccols(c)],
            cr_send.at[s, c, k], cr_recv.at[s, c, me_r],
        )

    def col_reduce_in(s, c, k):
        p = peer("row", k)
        slot = col_recv.at[s, p, :, ccols(c)]
        return copy("row", k, slot, slot, cr_send.at[s, c, k], cr_recv.at[s, c, p])

    def stat(axis, k, ref, me, send, recv):
        own = ref.at[me]
        return copy(axis, k, own, own, send.at[k], recv.at[me])

    def stat_in(axis, k, ref, send, recv):
        p = peer(axis, k)
        return copy(axis, k, ref.at[p], ref.at[p], send.at[k], recv.at[p])

    for c in range(ROW_CHUNKS):
        load(c).start()
    row_blk[0, me_c] = row_emb_in[...].astype(BF16)
    col_blk[0, me_r] = col_emb_in[...].astype(BF16)

    barrier = pltpu.get_barrier_semaphore()
    for k in range(1, n_row):
        pl.semaphore_signal(barrier, inc=1, device_id={"row": peer("row", k)}, device_id_type=MESH)
    for k in range(1, n_col):
        pl.semaphore_signal(barrier, inc=1, device_id={"col": peer("col", k)}, device_id_type=MESH)
    pl.semaphore_wait(barrier, n_row + n_col - 2)

    for c in range(ROW_CHUNKS):
        for k in range(1, n_col):
            row_gather(0, c, k).start()
    for c in range(COL_CHUNKS):
        for k in range(1, n_row):
            col_gather(0, c, k).start()

    def count_chunk(c, sums):
        load(c).wait()
        rows = rcols(c)
        rsum = jnp.zeros((8, cr), F32)
        new = []
        for t in range(COL_CHUNKS):
            cols = pl.ds(t * cc, cc)
            v = counts[rows, cols].astype(F32)
            m = jnp.maximum(v, 1.0)
            base[rows, cols] = jnp.log(m)
            weight[rows, cols] = 0.1 + 0.25 * (v * lax.rsqrt(m))
            h = v.astype(BF16)
            new.append(sums[t] + jnp.dot(jnp.ones((8, cr), BF16), h, preferred_element_type=F32))
            rsum = rsum + lax.dot_general(
                jnp.ones((8, cc), BF16), h, (((1,), (1,)), ((), ())), preferred_element_type=F32
            )
        row_stat[me_c, :, rows] = rsum[0:1, :]
        return tuple(new)

    sums = lax.fori_loop(
        0, ROW_CHUNKS, count_chunk, tuple(jnp.zeros((8, cc), F32) for _ in range(COL_CHUNKS))
    )
    for t in range(COL_CHUNKS):
        col_stat[me_r, :, pl.ds(t * cc, cc)] = sums[t][0:1, :]
    for k in range(1, n_row):
        stat("row", k, col_stat, me_r, cs_send, cs_recv).start()
    for k in range(1, n_col):
        stat("col", k, row_stat, me_c, rs_send, rs_recv).start()
    for k in range(1, n_row):
        stat_in("row", k, col_stat, cs_send, cs_recv).wait_recv()
    col_marg = jnp.sum(col_stat[...], axis=0)
    tot_stat[me_c] = jnp.broadcast_to(jnp.sum(col_marg, axis=1, keepdims=True), (1, 128))
    for k in range(1, n_col):
        stat("col", k, tot_stat, me_c, ts_send, ts_recv).start()
    for k in range(1, n_col):
        stat_in("col", k, row_stat, rs_send, rs_recv).wait_recv()
    log_row = jnp.log(jnp.sum(row_stat[...], axis=0))
    row_shift[...] = jnp.transpose(jnp.broadcast_to(log_row, (128, br)))
    for k in range(1, n_col):
        stat_in("col", k, tot_stat, ts_send, ts_recv).wait_recv()
    log_total = jnp.log(jnp.sum(tot_stat[...], axis=0))
    col_shift[...] = jnp.log(col_marg) - jnp.concatenate([log_total] * (bc // 128), axis=1)

    for s in range(SWEEPS):
        last = s == SWEEPS - 1
        row_emb = row_emb_in if s == 0 else row_out
        col_emb = col_emb_in if s == 0 else col_out
        row_accum = row_acc_in if s == 0 else row_acc
        col_accum = col_acc_in if s == 0 else col_acc

        for c in range(COL_CHUNKS):
            for k in range(1, n_row):
                col_gather_in(s, c, k).wait_recv()

        def grad_chunk(c, carry):
            rows = rcols(c)
            for k in range(1, n_col):
                row_gather_in(s, c, k).wait_recv()
            row_half = row_blk[s, :, :, rows].reshape(d, cr)
            shift = jnp.concatenate([row_shift[rows, :]] * (cc // 128), axis=1)
            row_grad = jnp.zeros((d, cr), F32)
            for t in range(COL_CHUNKS):
                cols = pl.ds(t * cc, cc)
                col_half = col_blk[s, :, :, cols].reshape(d, cc)
                scores = lax.dot_general(
                    row_half, col_half, (((0,), (0,)), ((), ())), preferred_element_type=F32
                )
                errors = scores - (base[rows, cols] - (shift + col_shift[:, cols]))
                w = weight[rows, cols]
                g = jnp.where(w > 0.2, w * errors, 0.5 * jnp.tanh(0.5 * errors) + 0.5).astype(BF16)
                grads[rows, cols] = g
                row_grad = row_grad + lax.dot_general(
                    col_half, g, (((1,), (1,)), ((), ())), preferred_element_type=F32
                )
            part = row_grad.astype(BF16).reshape(n_col, dr, cr)
            row_part[s, :, :, rows] = part
            row_recv[s, me_c, :, rows] = row_part[s, me_c, :, rows]
            for k in range(1, n_col):
                row_reduce(s, c, k).start()
            return carry

        lax.fori_loop(0, ROW_CHUNKS, grad_chunk, 0)

        def col_chunk(c, carry):
            cols = ccols(c)
            col_grad = jnp.dot(
                row_blk[s].reshape(d, br), grads[:, cols], preferred_element_type=F32
            )
            col_part[s, :, :, cols] = col_grad.astype(BF16).reshape(n_row, dc, cc)
            col_recv[s, me_r, :, cols] = col_part[s, me_r, :, cols]
            for k in range(1, n_row):
                col_reduce(s, c, k).start()
            return carry

        lax.fori_loop(0, COL_CHUNKS, col_chunk, 0)

        def row_update(c, carry):
            rows = rcols(c)
            for k in range(1, n_col):
                row_reduce_in(s, c, k).wait_recv()
            g = jnp.sum(row_recv[s, :, :, rows].astype(F32), axis=0)
            a = row_accum[:, rows] + g * g
            e = row_emb[:, rows] - 0.05 * g * lax.rsqrt(a)
            row_out[:, rows] = e
            if not last:
                row_acc[:, rows] = a
                row_blk[s + 1, me_c, :, rows] = e.astype(BF16)
                for k in range(1, n_col):
                    row_gather(s + 1, c, k).start()
            return carry

        def col_update(c, carry):
            cols = ccols(c)
            for k in range(1, n_row):
                col_reduce_in(s, c, k).wait_recv()
            g = jnp.sum(col_recv[s, :, :, cols].astype(F32), axis=0)
            a = col_accum[:, cols] + g * g
            e = col_emb[:, cols] - 0.05 * g * lax.rsqrt(a)
            col_out[:, cols] = e
            if not last:
                col_acc[:, cols] = a
                col_blk[s + 1, me_r, :, cols] = e.astype(BF16)
                for k in range(1, n_row):
                    col_gather(s + 1, c, k).start()
            return carry

        lax.fori_loop(0, ROW_CHUNKS, row_update, 0)
        lax.fori_loop(0, COL_CHUNKS, col_update, 0)

    for k in range(1, n_row):
        stat("row", k, col_stat, me_r, cs_send, cs_recv).wait_send()
    for k in range(1, n_col):
        stat("col", k, row_stat, me_c, rs_send, rs_recv).wait_send()
        stat("col", k, tot_stat, me_c, ts_send, ts_recv).wait_send()
    for s in range(SWEEPS):
        for c in range(ROW_CHUNKS):
            for k in range(1, n_col):
                row_gather(s, c, k).wait_send()
                row_reduce(s, c, k).wait_send()
        for c in range(COL_CHUNKS):
            for k in range(1, n_row):
                col_gather(s, c, k).wait_send()
                col_reduce(s, c, k).wait_send()


def on_device(n_row, n_col, counts, row_emb, col_emb, row_accum, col_accum):
    br, bc = counts.shape
    dr, dc = row_emb.shape[0], col_emb.shape[0]
    dma = pltpu.SemaphoreType.DMA
    vmem = pl.BlockSpec(memory_space=pltpu.VMEM)
    return pl.pallas_call(
        functools.partial(kernel, n_row, n_col),
        out_shape=(
            jax.ShapeDtypeStruct(row_emb.shape, F32),
            jax.ShapeDtypeStruct(col_emb.shape, F32),
        ),
        in_specs=[pl.BlockSpec(memory_space=pl.ANY), vmem, vmem, vmem, vmem],
        out_specs=(vmem, vmem),
        scratch_shapes=[
            pltpu.VMEM((br, bc), jnp.int32),
            pltpu.VMEM((br, bc), F32),
            pltpu.VMEM((br, bc), F32),
            pltpu.VMEM((br, bc), BF16),
            pltpu.VMEM((br, 128), F32),
            pltpu.VMEM((1, bc), F32),
            pltpu.VMEM((n_col, 1, br), F32),
            pltpu.VMEM((n_row, 1, bc), F32),
            pltpu.VMEM((n_col, 1, 128), F32),
            pltpu.VMEM((SWEEPS, n_col, dr, br), BF16),
            pltpu.VMEM((SWEEPS, n_row, dc, bc), BF16),
            pltpu.VMEM((SWEEPS, n_col, dr, br), BF16),
            pltpu.VMEM((SWEEPS, n_row, dc, bc), BF16),
            pltpu.VMEM((SWEEPS, n_col, dr, br), BF16),
            pltpu.VMEM((SWEEPS, n_row, dc, bc), BF16),
            pltpu.VMEM((dr, br), F32),
            pltpu.VMEM((dc, bc), F32),
            dma((ROW_CHUNKS,)),
            dma((n_col,)),
            dma((n_col,)),
            dma((n_row,)),
            dma((n_row,)),
            dma((n_col,)),
            dma((n_col,)),
            dma((SWEEPS, ROW_CHUNKS, n_col)),
            dma((SWEEPS, ROW_CHUNKS, n_col)),
            dma((SWEEPS, COL_CHUNKS, n_row)),
            dma((SWEEPS, COL_CHUNKS, n_row)),
            dma((SWEEPS, ROW_CHUNKS, n_col)),
            dma((SWEEPS, ROW_CHUNKS, n_col)),
            dma((SWEEPS, COL_CHUNKS, n_row)),
            dma((SWEEPS, COL_CHUNKS, n_row)),
        ],
        compiler_params=pltpu.CompilerParams(
            collective_id=0, has_side_effects=True, vmem_limit_bytes=56 * 1024 * 1024
        ),
    )(counts, row_emb, col_emb, row_accum, col_accum)


def solution(mesh):
    in_specs = (P("row", "col"), P("col", "row"), P("row", "col"), P("col", "row"), P("row", "col"))
    out_specs = (P("col", "row"), P("row", "col"))
    return jax.shard_map(
        functools.partial(on_device, mesh.shape["row"], mesh.shape["col"]),
        mesh=mesh, in_specs=in_specs, out_specs=out_specs, check_vma=False,
    )
```

```python
import functools

import jax
import jax.numpy as jnp
from jax import lax
from jax.experimental import pallas as pl
from jax.experimental.pallas import tpu as pltpu
from jax.sharding import PartitionSpec as P

SWEEPS = 2
ROW_CHUNKS = 4
COL_CHUNKS = 4
MESH = pl.DeviceIdType.MESH
F32 = jnp.float32
BF16 = jnp.bfloat16


def kernel(
    n_row, n_col, counts_hbm, row_emb_in, col_emb_in, row_acc_in, col_acc_in, row_out, col_out,
    counts, base, weight, grads, row_shift, col_shift, row_stat, col_stat, tot_stat,
    row_blk, col_blk, row_part, col_part, pair_recv, col_sum, row_recv, col_recv, row_acc, col_acc,
    load_sem, rs_send, rs_recv, cs_send, cs_recv, ts_send, ts_recv,
    rg_send, rg_recv, rf_send, cg_send, cg_recv, cf_send, rr_send, rr_recv,
    pr_send, pr_recv, cr_send, cr_recv,
):
    me_r, me_c = lax.axis_index("row"), lax.axis_index("col")
    br, bc = counts.shape
    dr, dc = row_emb_in.shape[0], col_emb_in.shape[0]
    d = dr * n_col
    cr, cc = br // ROW_CHUNKS, bc // COL_CHUNKS
    chips, side = n_row // 2, lax.rem(me_r, 2)
    other = 1 - side
    me_q = lax.div(me_r, 2)
    sibling = 2 * me_q + other
    first, end = 0, n_col - 1

    def peer(axis, k):
        return lax.rem(me_r + k, n_row) if axis == "row" else lax.rem(me_c + k, n_col)

    def copy(axis, k, src, dst, send_sem, recv_sem):
        return pltpu.make_async_remote_copy(
            src_ref=src, dst_ref=dst, send_sem=send_sem, recv_sem=recv_sem,
            device_id={axis: peer(axis, k)}, device_id_type=MESH,
        )

    def load(c):
        rows = pl.ds(pl.multiple_of(c * cr, cr), cr)
        return pltpu.make_async_copy(counts_hbm.at[rows, :], counts.at[rows, :], load_sem.at[c])

    def rcols(c):
        return pl.ds(pl.multiple_of(c * cr, cr), cr)

    def ccols(c):
        return pl.ds(pl.multiple_of(c * cc, cc), cc)

    def row_gather(s, c, k):
        own = row_blk.at[s, me_c, :, rcols(c)]
        return copy("col", k, own, own, rg_send.at[s, c, k], rg_recv.at[s, c, me_c])

    def row_gather_in(s, c, k):
        p = peer("col", k)
        slot = row_blk.at[s, p, :, rcols(c)]
        return copy("col", k, slot, slot, rg_send.at[s, c, k], rg_recv.at[s, c, p])

    def row_far(k):
        if k == 1:
            return me_c != end
        if k == n_col - 1:
            return me_c != first
        return None

    def row_gather_all(s, c, start):
        for k in range(1, n_col):
            go = row_gather(s, c, k).start if start else row_gather(s, c, k).wait_send
            if row_far(k) is None:
                go()
            else:
                pl.when(row_far(k))(go)

    def row_pass(s, c, to_end):
        slot = row_blk.at[s, first if to_end else end, :, rcols(c)]
        return copy(
            "col", 1 if to_end else n_col - 1, slot, slot,
            rf_send.at[s, c, int(to_end)], rg_recv.at[s, c, first if to_end else end],
        )

    def row_relay(s, c):
        @pl.when(me_c == end - 1)
        def _():
            row_gather_in(s, c, 2).wait_recv()
            row_pass(s, c, True).start()

        @pl.when(me_c == first + 1)
        def _():
            row_gather_in(s, c, n_col - 2).wait_recv()
            row_pass(s, c, False).start()

    def row_rest(s, c):
        for k in range(1, n_col):
            wait = row_gather_in(s, c, k).wait_recv
            here = None
            if k == 2:
                here = me_c != end - 1
            if k == n_col - 2:
                here = me_c != first + 1 if here is None else here & (me_c != first + 1)
            if here is None:
                wait()
            else:
                pl.when(here)(wait)

    def chip(k):
        return lax.rem(me_q + k, chips)

    def put(p, src, dst, send_sem, recv_sem):
        return pltpu.make_async_remote_copy(
            src_ref=src, dst_ref=dst, send_sem=send_sem, recv_sem=recv_sem,
            device_id={"row": p}, device_id_type=MESH,
        )

    def col_gather(s, c, k):
        own = col_blk.at[s, me_r, :, ccols(c)]
        p = sibling if k == 0 else 2 * chip(k) + side
        return put(p, own, own, cg_send.at[s, c, k], cg_recv.at[s, c, me_r])

    def col_gather_in(s, c, k, at):
        p = 2 * chip(k) + at
        slot = col_blk.at[s, p, :, ccols(c)]
        return put(sibling, slot, slot, cg_send.at[s, c, k], cg_recv.at[s, c, p])

    def col_pass(s, c, k):
        p = 2 * chip(k) + side
        slot = col_blk.at[s, p, :, ccols(c)]
        return put(sibling, slot, slot, cf_send.at[s, c, k], cg_recv.at[s, c, p])

    def col_relay(s, c):
        for k in range(1, chips):
            col_gather_in(s, c, k, side).wait_recv()
            col_pass(s, c, k).start()

    def col_rest(s, c):
        for k in range(chips):
            col_gather_in(s, c, k, other).wait_recv()

    def row_reduce(s, c, k):
        return copy(
            "col", k, row_part.at[s, peer("col", k), :, rcols(c)], row_recv.at[s, me_c, :, rcols(c)],
            rr_send.at[s, c, k], rr_recv.at[s, c, me_c],
        )

    def row_reduce_in(s, c, k):
        p = peer("col", k)
        slot = row_recv.at[s, p, :, rcols(c)]
        return copy("col", k, slot, slot, rr_send.at[s, c, k], rr_recv.at[s, c, p])

    def pair_reduce(s, c):
        return put(
            sibling, col_part.at[s, other, :, :, ccols(c)], pair_recv.at[s, :, :, ccols(c)],
            pr_send.at[s, c], pr_recv.at[s, c],
        )

    def col_reduce(s, c, k):
        return put(
            2 * chip(k) + side, col_sum.at[s, chip(k), :, ccols(c)], col_recv.at[s, me_q, :, ccols(c)],
            cr_send.at[s, c, k], cr_recv.at[s, c, me_q],
        )

    def col_reduce_in(s, c, k):
        slot = col_recv.at[s, chip(k), :, ccols(c)]
        return put(2 * chip(k) + side, slot, slot, cr_send.at[s, c, k], cr_recv.at[s, c, chip(k)])

    def stat(axis, k, ref, me, send, recv):
        own = ref.at[me]
        return copy(axis, k, own, own, send.at[k], recv.at[me])

    def stat_in(axis, k, ref, send, recv):
        p = peer(axis, k)
        return copy(axis, k, ref.at[p], ref.at[p], send.at[k], recv.at[p])

    for c in range(ROW_CHUNKS):
        load(c).start()
    row_blk[0, me_c] = row_emb_in[...].astype(BF16)
    col_blk[0, me_r] = col_emb_in[...].astype(BF16)

    barrier = pltpu.get_barrier_semaphore()
    for k in range(1, n_row):
        pl.semaphore_signal(barrier, inc=1, device_id={"row": peer("row", k)}, device_id_type=MESH)
    for k in range(1, n_col):
        pl.semaphore_signal(barrier, inc=1, device_id={"col": peer("col", k)}, device_id_type=MESH)
    pl.semaphore_wait(barrier, n_row + n_col - 2)

    for c in range(ROW_CHUNKS):
        row_gather_all(0, c, True)
    for c in range(COL_CHUNKS):
        for k in range(chips):
            col_gather(0, c, k).start()

    def count_chunk(c, sums):
        load(c).wait()
        rows = rcols(c)
        rsum = jnp.zeros((8, cr), F32)
        new = []
        for t in range(COL_CHUNKS):
            cols = pl.ds(t * cc, cc)
            v = counts[rows, cols].astype(F32)
            m = jnp.maximum(v, 1.0)
            base[rows, cols] = jnp.log(m)
            weight[rows, cols] = 0.1 + 0.25 * (v * lax.rsqrt(m))
            h = v.astype(BF16)
            new.append(sums[t] + jnp.dot(jnp.ones((8, cr), BF16), h, preferred_element_type=F32))
            rsum = rsum + lax.dot_general(
                jnp.ones((8, cc), BF16), h, (((1,), (1,)), ((), ())), preferred_element_type=F32
            )
        row_stat[me_c, :, rows] = rsum[0:1, :]
        return tuple(new)

    sums = lax.fori_loop(
        0, ROW_CHUNKS, count_chunk, tuple(jnp.zeros((8, cc), F32) for _ in range(COL_CHUNKS))
    )
    for t in range(COL_CHUNKS):
        col_stat[me_r, :, pl.ds(t * cc, cc)] = sums[t][0:1, :]
    for k in range(1, n_row):
        stat("row", k, col_stat, me_r, cs_send, cs_recv).start()
    for k in range(1, n_col):
        stat("col", k, row_stat, me_c, rs_send, rs_recv).start()
    for c in range(COL_CHUNKS // 2):
        col_relay(0, c)
    for k in range(1, n_row):
        stat_in("row", k, col_stat, cs_send, cs_recv).wait_recv()
    col_marg = jnp.sum(col_stat[...], axis=0)
    tot_stat[me_c] = jnp.broadcast_to(jnp.sum(col_marg, axis=1, keepdims=True), (1, 128))
    for k in range(1, n_col):
        stat("col", k, tot_stat, me_c, ts_send, ts_recv).start()
    for c in range(ROW_CHUNKS):
        row_relay(0, c)
    for c in range(COL_CHUNKS // 2, COL_CHUNKS):
        col_relay(0, c)
    for k in range(1, n_col):
        stat_in("col", k, row_stat, rs_send, rs_recv).wait_recv()
    log_row = jnp.log(jnp.sum(row_stat[...], axis=0))
    row_shift[...] = jnp.transpose(jnp.broadcast_to(log_row, (128, br)))
    for k in range(1, n_col):
        stat_in("col", k, tot_stat, ts_send, ts_recv).wait_recv()
    log_total = jnp.log(jnp.sum(tot_stat[...], axis=0))
    col_shift[...] = jnp.log(col_marg) - jnp.concatenate([log_total] * (bc // 128), axis=1)

    for s in range(SWEEPS):
        last = s == SWEEPS - 1
        row_emb = row_emb_in if s == 0 else row_out
        col_emb = col_emb_in if s == 0 else col_out
        row_accum = row_acc_in if s == 0 else row_acc
        col_accum = col_acc_in if s == 0 else col_acc

        for c in range(COL_CHUNKS):
            col_rest(s, c)

        def grad_chunk(c, carry):
            rows = rcols(c)
            row_rest(s, c)
            row_half = row_blk[s, :, :, rows].reshape(d, cr)
            shift = jnp.concatenate([row_shift[rows, :]] * (cc // 128), axis=1)
            row_grad = jnp.zeros((d, cr), F32)
            for t in range(COL_CHUNKS):
                cols = pl.ds(t * cc, cc)
                col_half = col_blk[s, :, :, cols].reshape(d, cc)
                scores = lax.dot_general(
                    row_half, col_half, (((0,), (0,)), ((), ())), preferred_element_type=F32
                )
                errors = scores - (base[rows, cols] - (shift + col_shift[:, cols]))
                w = weight[rows, cols]
                g = jnp.where(w > 0.2, w * errors, 0.5 * jnp.tanh(0.5 * errors) + 0.5).astype(BF16)
                grads[rows, cols] = g
                row_grad = row_grad + lax.dot_general(
                    col_half, g, (((1,), (1,)), ((), ())), preferred_element_type=F32
                )
            part = row_grad.astype(BF16).reshape(n_col, dr, cr)
            row_part[s, :, :, rows] = part
            row_recv[s, me_c, :, rows] = row_part[s, me_c, :, rows]
            for k in range(1, n_col):
                row_reduce(s, c, k).start()
            return carry

        lax.fori_loop(0, ROW_CHUNKS, grad_chunk, 0)

        def col_chunk(c, carry):
            cols = ccols(c)
            col_grad = jnp.dot(
                row_blk[s].reshape(d, br), grads[:, cols], preferred_element_type=F32
            )
            part = col_grad.astype(BF16).reshape(chips, 2, dc, cc)
            for h in range(2):
                col_part[s, h, :, :, cols] = part[:, h]
            pair_reduce(s, c).start()
            return carry

        lax.fori_loop(0, COL_CHUNKS, col_chunk, 0)

        def pair_chunk(c, carry):
            cols = ccols(c)
            pair_reduce(s, c).wait_recv()
            both = col_part[s, side, :, :, cols].astype(F32) + pair_recv[s, :, :, cols].astype(F32)
            col_sum[s, :, :, cols] = both.astype(BF16)
            for k in range(1, chips):
                col_reduce(s, c, k).start()
            col_recv[s, me_q, :, cols] = col_sum[s, me_q, :, cols]
            return carry

        lax.fori_loop(0, COL_CHUNKS, pair_chunk, 0)

        def row_update(c, carry):
            rows = rcols(c)
            for k in range(1, n_col):
                row_reduce_in(s, c, k).wait_recv()
            g = jnp.sum(row_recv[s, :, :, rows].astype(F32), axis=0)
            a = row_accum[:, rows] + g * g
            e = row_emb[:, rows] - 0.05 * g * lax.rsqrt(a)
            row_out[:, rows] = e
            if not last:
                row_acc[:, rows] = a
                row_blk[s + 1, me_c, :, rows] = e.astype(BF16)
                row_gather_all(s + 1, c, True)
            return carry

        def col_update(c, carry):
            cols = ccols(c)
            for k in range(1, chips):
                col_reduce_in(s, c, k).wait_recv()
            g = jnp.sum(col_recv[s, :, :, cols].astype(F32), axis=0)
            a = col_accum[:, cols] + g * g
            e = col_emb[:, cols] - 0.05 * g * lax.rsqrt(a)
            col_out[:, cols] = e
            if not last:
                col_acc[:, cols] = a
                col_blk[s + 1, me_r, :, cols] = e.astype(BF16)
                for k in range(chips):
                    col_gather(s + 1, c, k).start()
            return carry

        lax.fori_loop(0, ROW_CHUNKS, row_update, 0)
        lax.fori_loop(0, COL_CHUNKS, col_update, 0)
        if not last:
            for c in range(ROW_CHUNKS):
                row_relay(s + 1, c)
            for c in range(COL_CHUNKS):
                col_relay(s + 1, c)

    for k in range(1, n_row):
        stat("row", k, col_stat, me_r, cs_send, cs_recv).wait_send()
    for k in range(1, n_col):
        stat("col", k, row_stat, me_c, rs_send, rs_recv).wait_send()
        stat("col", k, tot_stat, me_c, ts_send, ts_recv).wait_send()
    for s in range(SWEEPS):
        for c in range(ROW_CHUNKS):
            row_gather_all(s, c, False)
            pl.when(me_c == end - 1)(row_pass(s, c, True).wait_send)
            pl.when(me_c == first + 1)(row_pass(s, c, False).wait_send)
            for k in range(1, n_col):
                row_reduce(s, c, k).wait_send()
        for c in range(COL_CHUNKS):
            pair_reduce(s, c).wait_send()
            for k in range(chips):
                col_gather(s, c, k).wait_send()
            for k in range(1, chips):
                col_pass(s, c, k).wait_send()
                col_reduce(s, c, k).wait_send()


def on_device(n_row, n_col, counts, row_emb, col_emb, row_accum, col_accum):
    br, bc = counts.shape
    dr, dc = row_emb.shape[0], col_emb.shape[0]
    dma = pltpu.SemaphoreType.DMA
    vmem = pl.BlockSpec(memory_space=pltpu.VMEM)
    return pl.pallas_call(
        functools.partial(kernel, n_row, n_col),
        out_shape=(
            jax.ShapeDtypeStruct(row_emb.shape, F32),
            jax.ShapeDtypeStruct(col_emb.shape, F32),
        ),
        in_specs=[pl.BlockSpec(memory_space=pl.ANY), vmem, vmem, vmem, vmem],
        out_specs=(vmem, vmem),
        scratch_shapes=[
            pltpu.VMEM((br, bc), jnp.int32),
            pltpu.VMEM((br, bc), F32),
            pltpu.VMEM((br, bc), F32),
            pltpu.VMEM((br, bc), BF16),
            pltpu.VMEM((br, 128), F32),
            pltpu.VMEM((1, bc), F32),
            pltpu.VMEM((n_col, 1, br), F32),
            pltpu.VMEM((n_row, 1, bc), F32),
            pltpu.VMEM((n_col, 1, 128), F32),
            pltpu.VMEM((SWEEPS, n_col, dr, br), BF16),
            pltpu.VMEM((SWEEPS, n_row, dc, bc), BF16),
            pltpu.VMEM((SWEEPS, n_col, dr, br), BF16),
            pltpu.VMEM((SWEEPS, 2, n_row // 2, dc, bc), BF16),
            pltpu.VMEM((SWEEPS, n_row // 2, dc, bc), BF16),
            pltpu.VMEM((SWEEPS, n_row // 2, dc, bc), BF16),
            pltpu.VMEM((SWEEPS, n_col, dr, br), BF16),
            pltpu.VMEM((SWEEPS, n_row // 2, dc, bc), BF16),
            pltpu.VMEM((dr, br), F32),
            pltpu.VMEM((dc, bc), F32),
            dma((ROW_CHUNKS,)),
            dma((n_col,)),
            dma((n_col,)),
            dma((n_row,)),
            dma((n_row,)),
            dma((n_col,)),
            dma((n_col,)),
            dma((SWEEPS, ROW_CHUNKS, n_col)),
            dma((SWEEPS, ROW_CHUNKS, n_col)),
            dma((SWEEPS, ROW_CHUNKS, 2)),
            dma((SWEEPS, COL_CHUNKS, n_row // 2)),
            dma((SWEEPS, COL_CHUNKS, n_row)),
            dma((SWEEPS, COL_CHUNKS, n_row // 2)),
            dma((SWEEPS, ROW_CHUNKS, n_col)),
            dma((SWEEPS, ROW_CHUNKS, n_col)),
            dma((SWEEPS, COL_CHUNKS)),
            dma((SWEEPS, COL_CHUNKS)),
            dma((SWEEPS, COL_CHUNKS, n_row // 2)),
            dma((SWEEPS, COL_CHUNKS, n_row // 2)),
        ],
        compiler_params=pltpu.CompilerParams(
            collective_id=0, has_side_effects=True, vmem_limit_bytes=56 * 1024 * 1024
        ),
    )(counts, row_emb, col_emb, row_accum, col_accum)


def solution(mesh):
    in_specs = (P("row", "col"), P("col", "row"), P("row", "col"), P("col", "row"), P("row", "col"))
    out_specs = (P("col", "row"), P("row", "col"))
    return jax.shard_map(
        functools.partial(on_device, mesh.shape["row"], mesh.shape["col"]),
        mesh=mesh, in_specs=in_specs, out_specs=out_specs, check_vma=False,
    )
```
